32 devices in a mesh: tm: 8 (over y, x, core), space: 4 (over z).
Axes of the slice: x: 2, y: 2, z: 4, core: 2. Of those that a mesh axis runs over, the one named last changes fastest.
Arguments:
- eigvecs: bfloat16 [2, 3, 8, 2048, 256], P(None, None, 'tm', 'space'), may hold values from -0.125 to 0.125
- propagator: bfloat16 [2, 3, 8, 2048, 128], P(None, None, 'tm', 'space'), may hold values from -6 to 6
- elementals: bfloat16 [8, 8, 2, 256, 256], P('tm'), may hold values from -0.0017089844 to 0.0017089844
- sink_times: int32 [8, 16], P('tm'), may hold values from 0 to 7, as said below
- momenta: int32 [8, 16], P('tm'), may hold values from 0 to 7
Outputs:
- traces: float32 [2, 8, 16], P(None, 'tm')
The draws below stay inside these ranges and needn't reach their ends.
Inputs may be any that keep to these rules, and one draw needn't show every extreme that they name: (sink_times[t, k] - t) modulo 8 lies in 0 to 5 or equals 7; item 0 of every slice t has sink time (t + 4) modulo 8, item 1 has (t - 1) modulo 8.
All inputs are finite; a program needn't handle non-finite values.
Results may differ from the reference program's by a relative error of at most 0.0049.
Values may be sent and summed in bfloat16 or wider, within the bound.
No kernel may reach another device: no remote copies, remote signals or barrier semaphores. Data moves between devices by JAX's collectives and lax.ppermute only.
A program may use at most 64 MiB of HBM per device.

```python
import jax
import jax.numpy as jnp
from jax import lax

NVEC = 256
NC = 3
NMOM = 8
ITEMS_DEV = 16
SB = 128
NT = 8
SITES = 2048


def draw_sink_times(key, part):
    separation = jax.random.randint(jax.random.fold_in(key, 17), (NT, ITEMS_DEV), -1, NT // 2 + 2, dtype=jnp.int32)
    separation = separation.at[:, 0].set(NT // 2)
    separation = separation.at[:, 1].set(-1)
    anchor = jnp.arange(NT, dtype=jnp.int32)[:, None]
    return ((anchor + separation + NT) % NT).astype(jnp.int32)


def with_ends(drawn, stream_key, least, top_value):
    index_at = [jax.random.randint(jax.random.fold_in(stream_key, axis), (), 0, length) for axis, length in enumerate(drawn.shape)]
    widest = drawn.shape.index(max(drawn.shape))
    neighbour = index_at[:widest] + [(index_at[widest] + 1) % drawn.shape[widest]] + index_at[widest + 1:]
    return drawn.at[tuple(index_at)].set(least).at[tuple(neighbour)].set(top_value)


def block_levels(stream_key, dims, pieces, low, high):
    def one(dim, shards_of):
        draws = jax.random.uniform(jax.random.fold_in(jax.random.fold_in(stream_key, 6), dim), (shards_of,), jnp.float32, low / len(pieces), high / len(pieces))
        return jnp.repeat(jnp.exp(draws), dims[dim] // shards_of).reshape((-1,) + (1,) * (len(dims) - dim - 1))

    factor_of = one(*pieces[0])
    for cut in pieces[1:]:
        factor_of = factor_of * one(*cut)
    return factor_of


def centred(own_key, extent, deviation, bound, cuts=(), held_as=jnp.bfloat16):
    values = jax.random.normal(own_key, extent, jnp.float32) * deviation
    if len(cuts) > 0:
        values = block_levels(own_key, extent, cuts, -0.22, 0.18) * values
    return jnp.clip(values, min=-bound, max=bound).astype(held_as)


def setup_inputs(seed: int = 0) -> dict:
    splits = jax.random.split(jax.random.key(seed), 6)
    return {
        "eigvecs": centred(splits[0], (2, NC, NT, SITES, NVEC), ((6 * SITES) ** -0.5), 0.125, ((2, 8), (3, 4))),
        "propagator": centred(splits[1], (2, NC, NT, SITES, SB), 1.0, 6.0, ((2, 8), (3, 4))),
        "elementals": centred(splits[2], (NT, NMOM, 2, NVEC, NVEC), (0.35 / (NVEC * SB ** 0.5)), 0.0017089844, ((0, 8),)),
        "sink_times": draw_sink_times(jax.random.fold_in(splits[5], 71), 0),
        "momenta": with_ends(jax.random.randint(splits[4], (NT, ITEMS_DEV), 0, NMOM), jax.random.fold_in(splits[4], 1), 0, NMOM - 1).astype(jnp.int32),
    }


def project(index, eigvecs, propagator):
    vecs = lax.dynamic_index_in_dim(eigvecs, index, 2, keepdims=False).reshape(2, -1, NVEC)
    props = lax.dynamic_index_in_dim(propagator, index, 2, keepdims=False).reshape(2, -1, SB)
    real_part = jnp.dot(props[0].T, vecs[0], preferred_element_type=jnp.float32) + jnp.dot(props[1].T, vecs[1], preferred_element_type=jnp.float32)
    imag_part = jnp.dot(props[1].T, vecs[0], preferred_element_type=jnp.float32) - jnp.dot(props[0].T, vecs[1], preferred_element_type=jnp.float32)
    return jnp.stack([real_part, imag_part], axis=1).astype(jnp.bfloat16)


def reference(eigvecs, propagator, elementals, sink_times, momenta):
    perams = lax.map(lambda index: project(index, eigvecs, propagator), jnp.arange(NT, dtype=jnp.int32))
    flat_perams = perams.reshape(NT, -1)

    def contract(index):
        moments = elementals[index].astype(jnp.float32)
        tau_block = perams[index].astype(jnp.float32)
        expand = jnp.einsum("prab,sqb->prsqa", moments, tau_block)
        real_part = expand[:, 0, :, 0] - expand[:, 1, :, 1]
        imag_part = expand[:, 0, :, 1] + expand[:, 1, :, 0]
        mixed_terms = jnp.stack([real_part, imag_part], axis=2).astype(jnp.bfloat16)
        swapped = jnp.stack([mixed_terms[:, :, 1], -mixed_terms[:, :, 0]], axis=2)
        weights = jnp.stack([mixed_terms, swapped], axis=1).reshape(2 * NMOM, -1)
        tables = jnp.dot(weights, flat_perams.T, preferred_element_type=jnp.float32).reshape(NMOM, 2, NT)
        picked = tables[momenta[index], :, sink_times[index]]
        return picked.T

    result = lax.map(contract, jnp.arange(NT, dtype=jnp.int32))
    return jnp.transpose(result, (1, 0, 2))
```

```python
import functools

import jax
import jax.numpy as jnp
from jax import lax
from jax.experimental import pallas as pl
from jax.experimental.pallas import tpu as pltpu
from jax.sharding import PartitionSpec as P

MIB = 1 << 20


def project_kernel(vec_hbm, prop_hbm, keep_ref, send_ref, vec_buf, prop_buf, acc_ref, sems):
    colours = vec_buf.shape[1]
    vec_count = vec_buf.shape[-1]
    columns = prop_buf.shape[-1]
    half = columns // 2
    copies = []
    for c in range(colours):
        vec_copy = pltpu.make_async_copy(vec_hbm.at[:, c, 0], vec_buf.at[:, c], sems.at[0, c])
        prop_copy = pltpu.make_async_copy(prop_hbm.at[:, c, 0], prop_buf.at[:, c], sems.at[1, c])
        prop_copy.start()
        vec_copy.start()
        copies.append((vec_copy, prop_copy))
    for c in range(colours):
        for copy in copies[c]:
            copy.wait()
        lhs = jnp.concatenate([prop_buf[0, c], prop_buf[1, c]], axis=-1)
        rhs = jnp.concatenate([vec_buf[0, c], vec_buf[1, c]], axis=-1)
        part = lax.dot_general(
            lhs, rhs, (((0,), (0,)), ((), ())), preferred_element_type=jnp.float32
        )
        if c == 0:
            acc_ref[...] = part
        else:
            acc_ref[...] += part
    mine = lax.rem(lax.axis_index("space"), 2)
    for out_ref, which in ((send_ref, 1 - mine), (keep_ref, mine)):
        top = pl.ds(pl.multiple_of(which * half, half), half)
        low = pl.ds(pl.multiple_of(columns + which * half, half), half)
        out_ref[0] = acc_ref[top, :vec_count] + acc_ref[low, vec_count:]
        out_ref[1] = acc_ref[low, :vec_count] - acc_ref[top, vec_count:]


def project(eigvecs, propagator):
    _, colours, _, sites, vec_count = eigvecs.shape
    columns = propagator.shape[-1]
    out = jax.ShapeDtypeStruct((2, columns // 2, vec_count), jnp.float32)
    return pl.pallas_call(
        project_kernel,
        out_shape=(out, out),
        in_specs=[pl.BlockSpec(memory_space=pl.ANY)] * 2,
        out_specs=[pl.BlockSpec(memory_space=pltpu.VMEM)] * 2,
        scratch_shapes=[
            pltpu.VMEM((2, colours, sites, vec_count), jnp.bfloat16),
            pltpu.VMEM((2, colours, sites, columns), jnp.bfloat16),
            pltpu.VMEM((2 * columns, 2 * vec_count), jnp.float32),
            pltpu.SemaphoreType.DMA((2, colours)),
        ],
        compiler_params=pltpu.CompilerParams(vmem_limit_bytes=16 * MIB),
        name="project",
    )(eigvecs, propagator)


def mix_kernel(own_ref, other_ref, elem_ref, mixed_ref):
    momenta = elem_ref.shape[1]
    half = own_ref.shape[1]
    full = (own_ref[...] + other_ref[...]).astype(jnp.bfloat16)
    both = full.reshape(2 * half, full.shape[-1])
    for p in range(momenta):
        by_real, by_imag = (
            lax.dot_general(
                both, elem_ref[0, p, r], (((1,), (1,)), ((), ())), preferred_element_type=jnp.float32
            )
            for r in range(2)
        )
        mixed_ref[p, 0] = (by_real[:half] - by_imag[half:]).astype(jnp.bfloat16)
        mixed_ref[p, 1] = (by_imag[:half] + by_real[half:]).astype(jnp.bfloat16)


def mix(own, other, elementals):
    momenta = elementals.shape[1]
    size = own.size
    return pl.pallas_call(
        mix_kernel,
        out_shape=jax.ShapeDtypeStruct((momenta,) + own.shape, jnp.bfloat16),
        in_specs=[pl.BlockSpec(memory_space=pltpu.VMEM)] * 3,
        out_specs=pl.BlockSpec(memory_space=pltpu.VMEM),
        compiler_params=pltpu.CompilerParams(vmem_limit_bytes=16 * MIB),
        cost_estimate=pl.CostEstimate(
            flops=4 * momenta * size * own.shape[-1], bytes_accessed=8 * size, transcendentals=0
        ),
        name="mix",
    )(own, other, elementals)


def trace_kernel(orders, sink_ref, mom_ref, mixed_ref, *refs):
    groups, out_ref, sums_ref = refs[:-2], refs[-2], refs[-1]
    items = out_ref.shape[1]
    own_slice = lax.axis_index("tm")
    own_core = own_slice & 1

    def one(k, carry):
        p = mom_ref[0, k]
        away = sink_ref[0, k] ^ own_slice
        crossed = away & 1
        holder = own_core ^ crossed
        slots = []
        for order in orders:
            slot = 0
            for place, bit in enumerate(order):
                slot = slot + (((away >> bit) & 1) << place)
            slots.append(slot)
        slot = jnp.where(holder == 0, slots[0], slots[1])
        late = slot >> (len(orders[0]) - 1)
        inner = slot & ((1 << (len(orders[0]) - 1)) - 1)
        group = crossed * 2 + late
        mixed_real = mixed_ref[p, 0].astype(jnp.float32)
        mixed_imag = mixed_ref[p, 1].astype(jnp.float32)
        for g, ref in enumerate(groups):

            @pl.when(group == g)
            def _(ref=ref):
                real = ref[inner, 0].astype(jnp.float32)
                imag = ref[inner, 1].astype(jnp.float32)
                for o, value in enumerate(
                    (mixed_real * real + mixed_imag * imag, mixed_imag * real - mixed_real * imag)
                ):
                    rows, lanes = value.shape
                    value = jnp.sum(value.reshape(rows // 8, 8, lanes), axis=0)
                    value = sum(value[:, i * 128 : (i + 1) * 128] for i in range(lanes // 128))
                    sums_ref[o, k] = value

        return carry

    lax.fori_loop(0, items, one, 0)
    out_ref[...] = jnp.sum(sums_ref[...], axis=2)


def trace(orders, sink_times, momenta, mixed, groups):
    items = sink_times.shape[1]
    return pl.pallas_call(
        functools.partial(trace_kernel, orders),
        out_shape=jax.ShapeDtypeStruct((2, items, 128), jnp.float32),
        in_specs=[pl.BlockSpec(memory_space=pltpu.SMEM)] * 2
        + [pl.BlockSpec(memory_space=pltpu.VMEM)] * (1 + len(groups)),
        out_specs=pl.BlockSpec(memory_space=pltpu.VMEM),
        scratch_shapes=[pltpu.VMEM((2, items, 8, 128), jnp.float32)],
        compiler_params=pltpu.CompilerParams(vmem_limit_bytes=16 * MIB),
        name="trace",
    )(sink_times, momenta, mixed, *groups)


def by_exchanges(slice_count, space_count, eigvecs, propagator, elementals, sink_times, momenta):
    axes = ("tm", "space")
    slice_bits = slice_count.bit_length() - 1
    space_bits = space_count.bit_length() - 1
    orders = (tuple(range(1, slice_bits)), tuple(range(slice_bits - 1, 0, -1)))

    def exchange(value, partner):
        pairs = []
        for t in range(slice_count):
            for s in range(space_count):
                to_t, to_s = partner(t, s)
                pairs.append((t * space_count + s, to_t * space_count + to_s))
        return lax.ppermute(value, axes, pairs)

    def across(value, bit):
        return exchange(value, lambda t, s: (t, s ^ (1 << bit)))

    keep, send = project(eigvecs, propagator)
    own = keep + across(send, 0)
    blocks = own.astype(jnp.bfloat16)[None]
    total, other = own, jnp.zeros_like(own)
    for bit in range(1, space_bits):
        if bit > 1:
            total = total + other
        other = across(total, bit)
    for step in range(slice_bits - 1):
        arrived = exchange(blocks, lambda t, s: (t ^ (1 << orders[t & 1][step]), s))
        if step < slice_bits - 2:
            blocks = jnp.concatenate([blocks, arrived], axis=0)
    cross = lambda t, s: (t ^ 1, s)
    groups = [blocks, arrived, exchange(blocks, cross), exchange(arrived, cross)]
    mixed = mix(total, other, elementals)
    partial = trace(orders, sink_times, momenta, mixed, groups)
    for bit in range(space_bits):
        partial = partial + across(partial, bit)
    return jnp.sum(partial, axis=-1)[:, None, :]


def by_collectives(eigvecs, propagator, elementals, sink_times, momenta):
    vec_count = eigvecs.shape[-1]
    column_count = propagator.shape[-1]
    momentum_count = elementals.shape[1]
    vecs_flat = eigvecs.reshape(2, -1, vec_count)
    columns_both = jnp.concatenate([vecs_flat[0], vecs_flat[1]], axis=0)
    columns_swap = jnp.concatenate([-vecs_flat[1], vecs_flat[0]], axis=0)
    vec_both = jnp.stack([columns_both, columns_swap], axis=1)
    prop_cat = propagator.reshape(-1, column_count)
    moments = elementals[0]
    own_block = lax.psum_scatter(
        lax.dot_general(
            prop_cat, vec_both, (((0,), (0,)), ((), ())), preferred_element_type=jnp.float32
        ),
        "space",
        scatter_dimension=0,
        tiled=True,
    ).astype(jnp.bfloat16)
    expand = jnp.einsum("prab,sqb->prsqa", moments, own_block, preferred_element_type=jnp.float32)
    real_part = expand[:, 0, :, 0] - expand[:, 1, :, 1]
    imag_part = expand[:, 0, :, 1] + expand[:, 1, :, 0]
    mixed_terms = jnp.stack([real_part, imag_part], axis=2).astype(jnp.bfloat16)
    swapped = jnp.stack([mixed_terms[:, :, 1], -mixed_terms[:, :, 0]], axis=2)
    weights = jnp.stack([mixed_terms, swapped], axis=1).reshape(2 * momentum_count, -1)
    time_slots = lax.axis_size("tm")
    pick_mom = (momenta[0][:, None] == jnp.arange(momentum_count, dtype=jnp.int32)[None, :]).astype(
        jnp.float32
    )
    blocks = lax.all_gather(own_block[None], "tm", axis=0, tiled=True)
    flattened = blocks.reshape(blocks.shape[0], -1)
    tables = lax.dot_general(
        weights, flattened, (((1,), (1,)), ((), ())), preferred_element_type=jnp.float32
    )
    slot_index = sink_times[0]
    tables = tables.reshape(momentum_count, 2, time_slots)
    pick_time = (slot_index[:, None] == jnp.arange(time_slots, dtype=jnp.int32)[None, :]).astype(
        jnp.float32
    )
    spread = jnp.einsum("kp,pot->okt", pick_mom, tables, precision=lax.Precision.HIGHEST)
    picked = jnp.sum(spread * pick_time[None], axis=2)
    summed = lax.psum(picked, "space")
    return summed[:, None, :]


def power_of_two(count):
    return count & (count - 1) == 0


def solution(mesh):
    slice_count, space_count = mesh.shape["tm"], mesh.shape["space"]
    on_device = by_collectives
    if power_of_two(slice_count) and power_of_two(space_count):
        if slice_count > 4 and space_count > 2:
            on_device = functools.partial(by_exchanges, slice_count, space_count)
    return jax.shard_map(
        on_device,
        mesh=mesh,
        in_specs=(
            P(None, None, "tm", "space", None),
            P(None, None, "tm", "space", None),
            P("tm", None, None, None, None),
            P("tm", None),
            P("tm", None),
        ),
        out_specs=P(None, "tm", None),
        check_vma=False,
    )
```

```python
import functools

import jax
import jax.numpy as jnp
from jax import lax
from jax.experimental import pallas as pl
from jax.experimental.pallas import tpu as pltpu
from jax.sharding import PartitionSpec as P

MIB = 1 << 20


def project_kernel(vec_hbm, prop_hbm, keep_ref, send_ref, vec_buf, prop_buf, acc_ref, sems):
    colours = vec_buf.shape[1]
    vec_count = vec_buf.shape[-1]
    columns = prop_buf.shape[-1]
    half = columns // 2
    copies = []
    for c in range(colours):
        vec_copy = pltpu.make_async_copy(vec_hbm.at[:, c, 0], vec_buf.at[:, c], sems.at[0, c])
        prop_copy = pltpu.make_async_copy(prop_hbm.at[:, c, 0], prop_buf.at[:, c], sems.at[1, c])
        prop_copy.start()
        vec_copy.start()
        copies.append((vec_copy, prop_copy))
    for c in range(colours):
        for copy in copies[c]:
            copy.wait()
        lhs = jnp.concatenate([prop_buf[0, c], prop_buf[1, c]], axis=-1)
        rhs = jnp.concatenate([vec_buf[0, c], vec_buf[1, c]], axis=-1)
        part = lax.dot_general(
            lhs, rhs, (((0,), (0,)), ((), ())), preferred_element_type=jnp.float32
        )
        if c == 0:
            acc_ref[...] = part
        else:
            acc_ref[...] += part
    mine = lax.rem(lax.axis_index("space"), 2)
    for out_ref, which in ((send_ref, 1 - mine), (keep_ref, mine)):
        top = pl.ds(pl.multiple_of(which * half, half), half)
        low = pl.ds(pl.multiple_of(columns + which * half, half), half)
        out_ref[0] = acc_ref[top, :vec_count] + acc_ref[low, vec_count:]
        out_ref[1] = acc_ref[low, :vec_count] - acc_ref[top, vec_count:]


def project(eigvecs, propagator):
    _, colours, _, sites, vec_count = eigvecs.shape
    columns = propagator.shape[-1]
    out = jax.ShapeDtypeStruct((2, columns // 2, vec_count), jnp.float32)
    return pl.pallas_call(
        project_kernel,
        out_shape=(out, out),
        in_specs=[pl.BlockSpec(memory_space=pl.ANY)] * 2,
        out_specs=[pl.BlockSpec(memory_space=pltpu.VMEM)] * 2,
        scratch_shapes=[
            pltpu.VMEM((2, colours, sites, vec_count), jnp.bfloat16),
            pltpu.VMEM((2, colours, sites, columns), jnp.bfloat16),
            pltpu.VMEM((2 * columns, 2 * vec_count), jnp.float32),
            pltpu.SemaphoreType.DMA((2, colours)),
        ],
        compiler_params=pltpu.CompilerParams(vmem_limit_bytes=53 * MIB),
        name="project",
    )(eigvecs, propagator)


def rounded(value):
    return value.astype(jnp.bfloat16).astype(jnp.float32)


def mix_kernel(own_ref, other_ref, elem_ref, mixed_ref):
    momenta = elem_ref.shape[1]
    half = own_ref.shape[1]
    full = (own_ref[...] + other_ref[...]).astype(jnp.bfloat16)
    both = full.reshape(2 * half, full.shape[-1])
    for p in range(momenta):
        by_real, by_imag = (
            lax.dot_general(
                both, elem_ref[0, p, r], (((1,), (1,)), ((), ())), preferred_element_type=jnp.float32
            )
            for r in range(2)
        )
        mixed_ref[p, 0] = rounded(by_real[:half] - by_imag[half:])
        mixed_ref[p, 1] = rounded(by_imag[:half] + by_real[half:])


def mix(own, other, elementals):
    momenta = elementals.shape[1]
    size = own.size
    return pl.pallas_call(
        mix_kernel,
        out_shape=jax.ShapeDtypeStruct((momenta,) + own.shape, jnp.float32),
        in_specs=[pl.BlockSpec(memory_space=pltpu.VMEM)] * 3,
        out_specs=pl.BlockSpec(memory_space=pltpu.VMEM),
        compiler_params=pltpu.CompilerParams(vmem_limit_bytes=16 * MIB),
        cost_estimate=pl.CostEstimate(
            flops=4 * momenta * size * own.shape[-1], bytes_accessed=8 * size, transcendentals=0
        ),
        name="mix",
    )(own, other, elementals)


def trace_kernel(orders, sink_ref, mom_ref, mixed_ref, *refs):
    groups, out_ref, slices_ref, sums_ref = refs[:-3], refs[-3], refs[-2], refs[-1]
    items = out_ref.shape[1]
    per_group = groups[0].shape[0]
    own_slice = lax.axis_index("tm")
    own_core = own_slice & 1
    for g, ref in enumerate(groups):
        slices_ref[g * per_group : (g + 1) * per_group] = ref[...]
    for k in range(items):
        p = mom_ref[0, k]
        away = sink_ref[0, k] ^ own_slice
        crossed = away & 1
        slots = []
        for order in orders:
            slot = 0
            for place, bit in enumerate(order):
                slot = slot + (((away >> bit) & 1) << place)
            slots.append(slot)
        slot = jnp.where(own_core ^ crossed == 0, slots[0], slots[1])
        slot = slot + crossed * (2 * per_group)
        real = slices_ref[slot, 0].astype(jnp.float32)
        imag = slices_ref[slot, 1].astype(jnp.float32)
        mixed_real = mixed_ref[p, 0]
        mixed_imag = mixed_ref[p, 1]
        for o, value in enumerate(
            (mixed_real * real + mixed_imag * imag, mixed_imag * real - mixed_real * imag)
        ):
            rows, lanes = value.shape
            value = jnp.sum(value.reshape(rows // 8, 8, lanes), axis=0)
            sums_ref[o, k] = sum(value[:, i * 128 : (i + 1) * 128] for i in range(lanes // 128))
    out_ref[...] = jnp.sum(sums_ref[...], axis=2)


def trace(orders, sink_times, momenta, mixed, groups):
    items = sink_times.shape[1]
    per_group = groups[0].shape[0]
    return pl.pallas_call(
        functools.partial(trace_kernel, orders),
        out_shape=jax.ShapeDtypeStruct((2, items, 128), jnp.float32),
        in_specs=[pl.BlockSpec(memory_space=pltpu.SMEM)] * 2
        + [pl.BlockSpec(memory_space=pltpu.VMEM)] * (1 + len(groups)),
        out_specs=pl.BlockSpec(memory_space=pltpu.VMEM),
        scratch_shapes=[
            pltpu.VMEM((len(groups) * per_group,) + groups[0].shape[1:], jnp.bfloat16),
            pltpu.VMEM((2, items, 8, 128), jnp.float32),
        ],
        compiler_params=pltpu.CompilerParams(vmem_limit_bytes=16 * MIB),
        name="trace",
    )(sink_times, momenta, mixed, *groups)


def by_exchanges(slice_count, space_count, eigvecs, propagator, elementals, sink_times, momenta):
    axes = ("tm", "space")
    slice_bits = slice_count.bit_length() - 1
    space_bits = space_count.bit_length() - 1
    orders = (tuple(range(1, slice_bits)), tuple(range(slice_bits - 1, 0, -1)))

    def exchange(value, partner):
        pairs = []
        for t in range(slice_count):
            for s in range(space_count):
                to_t, to_s = partner(t, s)
                pairs.append((t * space_count + s, to_t * space_count + to_s))
        return lax.ppermute(value, axes, pairs)

    def across(value, bit):
        return exchange(value, lambda t, s: (t, s ^ (1 << bit)))

    keep, send = project(eigvecs, propagator)
    own = keep + across(send, 0)
    blocks = own.astype(jnp.bfloat16)[None]
    total, other = own, jnp.zeros_like(own)
    for bit in range(1, space_bits):
        if bit > 1:
            total = total + other
        other = across(total, bit)
    for step in range(slice_bits - 1):
        arrived = exchange(blocks, lambda t, s: (t ^ (1 << orders[t & 1][step]), s))
        if step < slice_bits - 2:
            blocks = jnp.concatenate([blocks, arrived], axis=0)
    arrived, other = lax.optimization_barrier((arrived, other))
    cross = lambda t, s: (t ^ 1, s)
    groups = [blocks, arrived, exchange(blocks, cross), exchange(arrived, cross)]
    mixed = mix(total, other, elementals)
    partial = trace(orders, sink_times, momenta, mixed, groups)
    for bit in range(space_bits):
        partial = partial + across(partial, bit)
    return jnp.sum(partial, axis=-1)[:, None, :]


def by_collectives(eigvecs, propagator, elementals, sink_times, momenta):
    vec_count = eigvecs.shape[-1]
    column_count = propagator.shape[-1]
    momentum_count = elementals.shape[1]
    vecs_flat = eigvecs.reshape(2, -1, vec_count)
    columns_both = jnp.concatenate([vecs_flat[0], vecs_flat[1]], axis=0)
    columns_swap = jnp.concatenate([-vecs_flat[1], vecs_flat[0]], axis=0)
    vec_both = jnp.stack([columns_both, columns_swap], axis=1)
    prop_cat = propagator.reshape(-1, column_count)
    moments = elementals[0]
    own_block = lax.psum_scatter(
        lax.dot_general(
            prop_cat, vec_both, (((0,), (0,)), ((), ())), preferred_element_type=jnp.float32
        ),
        "space",
        scatter_dimension=0,
        tiled=True,
    ).astype(jnp.bfloat16)
    expand = jnp.einsum("prab,sqb->prsqa", moments, own_block, preferred_element_type=jnp.float32)
    real_part = expand[:, 0, :, 0] - expand[:, 1, :, 1]
    imag_part = expand[:, 0, :, 1] + expand[:, 1, :, 0]
    mixed_terms = jnp.stack([real_part, imag_part], axis=2).astype(jnp.bfloat16)
    swapped = jnp.stack([mixed_terms[:, :, 1], -mixed_terms[:, :, 0]], axis=2)
    weights = jnp.stack([mixed_terms, swapped], axis=1).reshape(2 * momentum_count, -1)
    time_slots = lax.axis_size("tm")
    pick_mom = (momenta[0][:, None] == jnp.arange(momentum_count, dtype=jnp.int32)[None, :]).astype(
        jnp.float32
    )
    blocks = lax.all_gather(own_block[None], "tm", axis=0, tiled=True)
    flattened = blocks.reshape(blocks.shape[0], -1)
    tables = lax.dot_general(
        weights, flattened, (((1,), (1,)), ((), ())), preferred_element_type=jnp.float32
    )
    slot_index = sink_times[0]
    tables = tables.reshape(momentum_count, 2, time_slots)
    pick_time = (slot_index[:, None] == jnp.arange(time_slots, dtype=jnp.int32)[None, :]).astype(
        jnp.float32
    )
    spread = jnp.einsum("kp,pot->okt", pick_mom, tables, precision=lax.Precision.HIGHEST)
    picked = jnp.sum(spread * pick_time[None], axis=2)
    summed = lax.psum(picked, "space")
    return summed[:, None, :]


def power_of_two(count):
    return count & (count - 1) == 0


def solution(mesh):
    slice_count, space_count = mesh.shape["tm"], mesh.shape["space"]
    on_device = by_collectives
    if power_of_two(slice_count) and power_of_two(space_count):
        if slice_count > 4 and space_count > 2:
            on_device = functools.partial(by_exchanges, slice_count, space_count)
    return jax.shard_map(
        on_device,
        mesh=mesh,
        in_specs=(
            P(None, None, "tm", "space", None),
            P(None, None, "tm", "space", None),
            P("tm", None, None, None, None),
            P("tm", None),
            P("tm", None),
        ),
        out_specs=P(None, "tm", None),
        check_vma=False,
    )
```

```python
import functools

import jax
import jax.numpy as jnp
from jax import lax
from jax.experimental import pallas as pl
from jax.experimental.pallas import tpu as pltpu
from jax.sharding import PartitionSpec as P

MIB = 1 << 20


def project_kernel(vec_hbm, prop_hbm, keep_ref, send_ref, vec_buf, prop_buf, acc_ref, sems):
    colours = vec_buf.shape[1]
    vec_count = vec_buf.shape[-1]
    columns = prop_buf.shape[-1]
    half = columns // 2
    copies = []
    for c in range(colours):
        vec_copy = pltpu.make_async_copy(vec_hbm.at[:, c, 0], vec_buf.at[:, c], sems.at[0, c])
        prop_copy = pltpu.make_async_copy(prop_hbm.at[:, c, 0], prop_buf.at[:, c], sems.at[1, c])
        prop_copy.start()
        vec_copy.start()
        copies.append((vec_copy, prop_copy))
    for c in range(colours):
        for copy in copies[c]:
            copy.wait()
        lhs = jnp.concatenate([prop_buf[0, c], prop_buf[1, c]], axis=-1)
        rhs = jnp.concatenate([vec_buf[0, c], vec_buf[1, c]], axis=-1)
        part = lax.dot_general(
            lhs, rhs, (((0,), (0,)), ((), ())), preferred_element_type=jnp.float32
        )
        if c == 0:
            acc_ref[...] = part
        else:
            acc_ref[...] += part
    mine = lax.rem(lax.axis_index("space"), 2)
    for out_ref, which in ((send_ref, 1 - mine), (keep_ref, mine)):
        top = pl.ds(pl.multiple_of(which * half, half), half)
        low = pl.ds(pl.multiple_of(columns + which * half, half), half)
        out_ref[0] = acc_ref[top, :vec_count] + acc_ref[low, vec_count:]
        out_ref[1] = acc_ref[low, :vec_count] - acc_ref[top, vec_count:]


def project(eigvecs, propagator):
    _, colours, _, sites, vec_count = eigvecs.shape
    columns = propagator.shape[-1]
    out = jax.ShapeDtypeStruct((2, columns // 2, vec_count), jnp.float32)
    return pl.pallas_call(
        project_kernel,
        out_shape=(out, out),
        in_specs=[pl.BlockSpec(memory_space=pl.ANY)] * 2,
        out_specs=[pl.BlockSpec(memory_space=pltpu.VMEM)] * 2,
        scratch_shapes=[
            pltpu.VMEM((2, colours, sites, vec_count), jnp.bfloat16),
            pltpu.VMEM((2, colours, sites, columns), jnp.bfloat16),
            pltpu.VMEM((2 * columns, 2 * vec_count), jnp.float32),
            pltpu.SemaphoreType.DMA((2, colours)),
        ],
        compiler_params=pltpu.CompilerParams(vmem_limit_bytes=53 * MIB),
        name="project",
    )(eigvecs, propagator)


def rounded(value):
    return value.astype(jnp.bfloat16).astype(jnp.float32)


def mix_kernel(own_ref, other_ref, elem_ref, mixed_ref):
    momenta = elem_ref.shape[1]
    half = own_ref.shape[1]
    full = (own_ref[...] + other_ref[...]).astype(jnp.bfloat16)
    both = full.reshape(2 * half, full.shape[-1])
    for p in range(momenta):
        by_real, by_imag = (
            lax.dot_general(
                both, elem_ref[0, p, r], (((1,), (1,)), ((), ())), preferred_element_type=jnp.float32
            )
            for r in range(2)
        )
        mixed_ref[p, 0] = rounded(by_real[:half] - by_imag[half:])
        mixed_ref[p, 1] = rounded(by_imag[:half] + by_real[half:])


def mix(own, other, elementals):
    momenta = elementals.shape[1]
    size = own.size
    return pl.pallas_call(
        mix_kernel,
        out_shape=jax.ShapeDtypeStruct((momenta,) + own.shape, jnp.float32),
        in_specs=[pl.BlockSpec(memory_space=pltpu.VMEM)] * 3,
        out_specs=pl.BlockSpec(memory_space=pltpu.VMEM),
        compiler_params=pltpu.CompilerParams(vmem_limit_bytes=16 * MIB),
        cost_estimate=pl.CostEstimate(
            flops=4 * momenta * size * own.shape[-1], bytes_accessed=8 * size, transcendentals=0
        ),
        name="mix",
    )(own, other, elementals)


def trace_kernel(orders, sink_ref, mom_ref, mixed_ref, *refs):
    groups, out_ref, slices_ref, sums_ref = refs[:-3], refs[-3], refs[-2], refs[-1]
    items = out_ref.shape[1]
    per_group = groups[0].shape[0]
    own_slice = lax.axis_index("tm")
    own_core = own_slice & 1
    for g, ref in enumerate(groups):
        slices_ref[g * per_group : (g + 1) * per_group] = ref[...]
    for k in range(items):
        p = mom_ref[0, k]
        away = sink_ref[0, k] ^ own_slice
        crossed = away & 1
        slots = []
        for order in orders:
            slot = 0
            for place, bit in enumerate(order):
                slot = slot + (((away >> bit) & 1) << place)
            slots.append(slot)
        slot = jnp.where(own_core ^ crossed == 0, slots[0], slots[1])
        crossed = crossed ^ (slot >> (len(orders[0]) - 1))
        slot = slot + crossed * (2 * per_group)
        real = slices_ref[slot, 0].astype(jnp.float32)
        imag = slices_ref[slot, 1].astype(jnp.float32)
        mixed_real = mixed_ref[p, 0]
        mixed_imag = mixed_ref[p, 1]
        for o, value in enumerate(
            (mixed_real * real + mixed_imag * imag, mixed_imag * real - mixed_real * imag)
        ):
            rows, lanes = value.shape
            value = jnp.sum(value.reshape(rows // 8, 8, lanes), axis=0)
            sums_ref[o, k] = sum(value[:, i * 128 : (i + 1) * 128] for i in range(lanes // 128))
    out_ref[...] = jnp.sum(sums_ref[...], axis=2)


def trace(orders, sink_times, momenta, mixed, groups):
    items = sink_times.shape[1]
    per_group = groups[0].shape[0]
    return pl.pallas_call(
        functools.partial(trace_kernel, orders),
        out_shape=jax.ShapeDtypeStruct((2, items, 128), jnp.float32),
        in_specs=[pl.BlockSpec(memory_space=pltpu.SMEM)] * 2
        + [pl.BlockSpec(memory_space=pltpu.VMEM)] * (1 + len(groups)),
        out_specs=pl.BlockSpec(memory_space=pltpu.VMEM),
        scratch_shapes=[
            pltpu.VMEM((len(groups) * per_group,) + groups[0].shape[1:], jnp.bfloat16),
            pltpu.VMEM((2, items, 8, 128), jnp.float32),
        ],
        compiler_params=pltpu.CompilerParams(vmem_limit_bytes=16 * MIB),
        name="trace",
    )(sink_times, momenta, mixed, *groups)


def by_exchanges(slice_count, space_count, eigvecs, propagator, elementals, sink_times, momenta):
    axes = ("tm", "space")
    slice_bits = slice_count.bit_length() - 1
    space_bits = space_count.bit_length() - 1
    orders = (tuple(range(1, slice_bits)), tuple(range(slice_bits - 1, 0, -1)))

    def exchange(value, partner):
        pairs = []
        for t in range(slice_count):
            for s in range(space_count):
                to_t, to_s = partner(t, s)
                pairs.append((t * space_count + s, to_t * space_count + to_s))
        return lax.ppermute(value, axes, pairs)

    def across(value, bit):
        return exchange(value, lambda t, s: (t, s ^ (1 << bit)))

    keep, send = project(eigvecs, propagator)
    own = keep + across(send, 0)
    blocks = own.astype(jnp.bfloat16)[None]
    total, other = own, jnp.zeros_like(own)
    for bit in range(1, space_bits):
        if bit > 1:
            total = total + other
        other = across(total, bit)
    for step in range(slice_bits - 1):
        flip = 1 if step == slice_bits - 2 else 0
        arrived = exchange(blocks, lambda t, s: (t ^ (1 << orders[t & 1][step]) ^ flip, s))
        if step < slice_bits - 2:
            blocks = jnp.concatenate([blocks, arrived], axis=0)
    arrived, other = lax.optimization_barrier((arrived, other))
    cross = lambda t, s: (t ^ 1, s)
    groups = [blocks, arrived, exchange(blocks, cross), exchange(arrived, cross)]
    mixed = mix(total, other, elementals)
    partial = trace(orders, sink_times, momenta, mixed, groups)
    for bit in range(space_bits):
        far = exchange(partial, lambda t, s: (t ^ 1, s ^ (1 << bit)))
        partial = far + exchange(partial, cross)
    return jnp.sum(partial, axis=-1)[:, None, :]


def by_collectives(eigvecs, propagator, elementals, sink_times, momenta):
    vec_count = eigvecs.shape[-1]
    column_count = propagator.shape[-1]
    momentum_count = elementals.shape[1]
    vecs_flat = eigvecs.reshape(2, -1, vec_count)
    columns_both = jnp.concatenate([vecs_flat[0], vecs_flat[1]], axis=0)
    columns_swap = jnp.concatenate([-vecs_flat[1], vecs_flat[0]], axis=0)
    vec_both = jnp.stack([columns_both, columns_swap], axis=1)
    prop_cat = propagator.reshape(-1, column_count)
    moments = elementals[0]
    own_block = lax.psum_scatter(
        lax.dot_general(
            prop_cat, vec_both, (((0,), (0,)), ((), ())), preferred_element_type=jnp.float32
        ),
        "space",
        scatter_dimension=0,
        tiled=True,
    ).astype(jnp.bfloat16)
    expand = jnp.einsum("prab,sqb->prsqa", moments, own_block, preferred_element_type=jnp.float32)
    real_part = expand[:, 0, :, 0] - expand[:, 1, :, 1]
    imag_part = expand[:, 0, :, 1] + expand[:, 1, :, 0]
    mixed_terms = jnp.stack([real_part, imag_part], axis=2).astype(jnp.bfloat16)
    swapped = jnp.stack([mixed_terms[:, :, 1], -mixed_terms[:, :, 0]], axis=2)
    weights = jnp.stack([mixed_terms, swapped], axis=1).reshape(2 * momentum_count, -1)
    time_slots = lax.axis_size("tm")
    pick_mom = (momenta[0][:, None] == jnp.arange(momentum_count, dtype=jnp.int32)[None, :]).astype(
        jnp.float32
    )
    blocks = lax.all_gather(own_block[None], "tm", axis=0, tiled=True)
    flattened = blocks.reshape(blocks.shape[0], -1)
    tables = lax.dot_general(
        weights, flattened, (((1,), (1,)), ((), ())), preferred_element_type=jnp.float32
    )
    slot_index = sink_times[0]
    tables = tables.reshape(momentum_count, 2, time_slots)
    pick_time = (slot_index[:, None] == jnp.arange(time_slots, dtype=jnp.int32)[None, :]).astype(
        jnp.float32
    )
    spread = jnp.einsum("kp,pot->okt", pick_mom, tables, precision=lax.Precision.HIGHEST)
    picked = jnp.sum(spread * pick_time[None], axis=2)
    summed = lax.psum(picked, "space")
    return summed[:, None, :]


def solution(mesh):
    slice_count, space_count = mesh.shape["tm"], mesh.shape["space"]
    slice_bits, space_bits = slice_count.bit_length() - 1, space_count.bit_length() - 1
    on_device = by_collectives
    if (slice_count, space_count) == (1 << slice_bits, 1 << space_bits):
        if slice_bits > 2 and space_bits > 0 and space_bits % 2 == 0:
            on_device = functools.partial(by_exchanges, slice_count, space_count)
    return jax.shard_map(
        on_device,
        mesh=mesh,
        in_specs=(
            P(None, None, "tm", "space", None),
            P(None, None, "tm", "space", None),
            P("tm", None, None, None, None),
            P("tm", None),
            P("tm", None),
        ),
        out_specs=P(None, "tm", None),
        check_vma=False,
    )
```

```python
import functools

import jax
import jax.numpy as jnp
from jax import lax
from jax.experimental import pallas as pl
from jax.experimental.pallas import tpu as pltpu
from jax.sharding import PartitionSpec as P

MIB = 1 << 20


def project_kernel(vec_hbm, prop_hbm, keep_ref, send_ref, vec_buf, prop_buf, acc_ref, sems):
    colours = vec_buf.shape[1]
    vec_count = vec_buf.shape[-1]
    columns = prop_buf.shape[-1]
    half = columns // 2
    copies = []
    for c in range(colours):
        vec_copy = pltpu.make_async_copy(vec_hbm.at[:, c, 0], vec_buf.at[:, c], sems.at[0, c])
        prop_copy = pltpu.make_async_copy(prop_hbm.at[:, c, 0], prop_buf.at[:, c], sems.at[1, c])
        prop_copy.start()
        vec_copy.start()
        copies.append((vec_copy, prop_copy))
    for c in range(colours):
        for copy in copies[c]:
            copy.wait()
        lhs = jnp.concatenate([prop_buf[0, c], prop_buf[1, c]], axis=-1)
        rhs = jnp.concatenate([vec_buf[0, c], vec_buf[1, c]], axis=-1)
        part = lax.dot_general(
            lhs, rhs, (((0,), (0,)), ((), ())), preferred_element_type=jnp.float32
        )
        if c == 0:
            acc_ref[...] = part
        else:
            acc_ref[...] += part
    mine = lax.rem(lax.axis_index("space"), 2)
    for out_ref, which in ((send_ref, 1 - mine), (keep_ref, mine)):
        top = pl.ds(pl.multiple_of(which * half, half), half)
        low = pl.ds(pl.multiple_of(columns + which * half, half), half)
        out_ref[0] = acc_ref[top, :vec_count] + acc_ref[low, vec_count:]
        out_ref[1] = acc_ref[low, :vec_count] - acc_ref[top, vec_count:]


def project(eigvecs, propagator):
    _, colours, _, sites, vec_count = eigvecs.shape
    columns = propagator.shape[-1]
    out = jax.ShapeDtypeStruct((2, columns // 2, vec_count), jnp.float32)
    return pl.pallas_call(
        project_kernel,
        out_shape=(out, out),
        in_specs=[pl.BlockSpec(memory_space=pl.ANY)] * 2,
        out_specs=[pl.BlockSpec(memory_space=pltpu.VMEM)] * 2,
        scratch_shapes=[
            pltpu.VMEM((2, colours, sites, vec_count), jnp.bfloat16),
            pltpu.VMEM((2, colours, sites, columns), jnp.bfloat16),
            pltpu.VMEM((2 * columns, 2 * vec_count), jnp.float32),
            pltpu.SemaphoreType.DMA((2, colours)),
        ],
        compiler_params=pltpu.CompilerParams(vmem_limit_bytes=53 * MIB),
        name="project",
    )(eigvecs, propagator)


def rounded(value):
    return value.astype(jnp.bfloat16).astype(jnp.float32)


def mix_kernel(own_ref, other_ref, elem_ref, mixed_ref):
    momenta = elem_ref.shape[1]
    half = own_ref.shape[1]
    full = (own_ref[...] + other_ref[...]).astype(jnp.bfloat16)
    both = full.reshape(2 * half, full.shape[-1])
    for p in range(momenta):
        by_real, by_imag = (
            lax.dot_general(
                both, elem_ref[0, p, r], (((1,), (1,)), ((), ())), preferred_element_type=jnp.float32
            )
            for r in range(2)
        )
        mixed_ref[p, 0] = rounded(by_real[:half] - by_imag[half:])
        mixed_ref[p, 1] = rounded(by_imag[:half] + by_real[half:])


def mix(own, other, elementals):
    momenta = elementals.shape[1]
    size = own.size
    return pl.pallas_call(
        mix_kernel,
        out_shape=jax.ShapeDtypeStruct((momenta,) + own.shape, jnp.float32),
        in_specs=[pl.BlockSpec(memory_space=pltpu.VMEM)] * 3,
        out_specs=pl.BlockSpec(memory_space=pltpu.VMEM),
        compiler_params=pltpu.CompilerParams(vmem_limit_bytes=16 * MIB),
        cost_estimate=pl.CostEstimate(
            flops=4 * momenta * size * own.shape[-1], bytes_accessed=8 * size, transcendentals=0
        ),
        name="mix",
    )(own, other, elementals)


def trace_kernel(orders, sink_ref, mom_ref, mixed_ref, *refs):
    groups, out_ref, slices_ref, sums_ref = refs[:-3], refs[-3], refs[-2], refs[-1]
    items = out_ref.shape[1]
    per_group = groups[0].shape[0]
    own_slice = lax.axis_index("tm")
    own_core = own_slice & 1
    for g, ref in enumerate(groups):
        slices_ref[g * per_group : (g + 1) * per_group] = ref[...]
    for k in range(items):
        p = mom_ref[0, k]
        away = sink_ref[0, k] ^ own_slice
        crossed = away & 1
        slots = []
        for order in orders:
            slot = 0
            for place, bit in enumerate(order):
                slot = slot + (((away >> bit) & 1) << place)
            slots.append(slot)
        slot = jnp.where(own_core ^ crossed == 0, slots[0], slots[1])
        crossed = crossed ^ (slot >> (len(orders[0]) - 1))
        slot = slot + crossed * (2 * per_group)
        real = slices_ref[slot, 0].astype(jnp.float32)
        imag = slices_ref[slot, 1].astype(jnp.float32)
        mixed_real = mixed_ref[p, 0]
        mixed_imag = mixed_ref[p, 1]
        for o, value in enumerate(
            (mixed_real * real + mixed_imag * imag, mixed_imag * real - mixed_real * imag)
        ):
            rows, lanes = value.shape
            value = jnp.sum(value.reshape(rows // 8, 8, lanes), axis=0)
            sums_ref[o, k] = sum(value[:, i * 128 : (i + 1) * 128] for i in range(lanes // 128))
    out_ref[...] = jnp.sum(jnp.sum(sums_ref[...], axis=2), axis=-1)


def trace(orders, sink_times, momenta, mixed, groups):
    items = sink_times.shape[1]
    per_group = groups[0].shape[0]
    return pl.pallas_call(
        functools.partial(trace_kernel, orders),
        out_shape=jax.ShapeDtypeStruct((2, items), jnp.float32),
        in_specs=[pl.BlockSpec(memory_space=pltpu.VMEM)] * (3 + len(groups)),
        out_specs=pl.BlockSpec(memory_space=pltpu.VMEM),
        scratch_shapes=[
            pltpu.VMEM((len(groups) * per_group,) + groups[0].shape[1:], jnp.bfloat16),
            pltpu.VMEM((2, items, 8, 128), jnp.float32),
        ],
        compiler_params=pltpu.CompilerParams(vmem_limit_bytes=16 * MIB),
        name="trace",
    )(sink_times, momenta, mixed, *groups)


def by_exchanges(slice_count, space_count, eigvecs, propagator, elementals, sink_times, momenta):
    axes = ("tm", "space")
    slice_bits = slice_count.bit_length() - 1
    space_bits = space_count.bit_length() - 1
    orders = (tuple(range(1, slice_bits)), tuple(range(slice_bits - 1, 0, -1)))

    def exchange(value, partner):
        pairs = []
        for t in range(slice_count):
            for s in range(space_count):
                to_t, to_s = partner(t, s)
                pairs.append((t * space_count + s, to_t * space_count + to_s))
        return lax.ppermute(value, axes, pairs)

    def across(value, bit):
        return exchange(value, lambda t, s: (t, s ^ (1 << bit)))

    keep, send = project(eigvecs, propagator)
    own = keep + across(send, 0)
    blocks = own.astype(jnp.bfloat16)[None]
    total, other = own, jnp.zeros_like(own)
    for bit in range(1, space_bits):
        if bit > 1:
            total = total + other
        other = across(total, bit)
    for step in range(slice_bits - 1):
        flip = 1 if step == slice_bits - 2 else 0
        arrived = exchange(blocks, lambda t, s: (t ^ (1 << orders[t & 1][step]) ^ flip, s))
        if step < slice_bits - 2:
            blocks = jnp.concatenate([blocks, arrived], axis=0)
    arrived, other = lax.optimization_barrier((arrived, other))
    cross = lambda t, s: (t ^ 1, s)
    groups = [blocks, arrived, exchange(blocks, cross), exchange(arrived, cross)]
    mixed = mix(total, other, elementals)
    partial = trace(orders, sink_times, momenta, mixed, groups)
    for bit in range(space_bits):
        far = exchange(partial, lambda t, s: (t ^ 1, s ^ (1 << bit)))
        partial = far + exchange(partial, cross)
    return partial[:, None, :]


def by_collectives(eigvecs, propagator, elementals, sink_times, momenta):
    vec_count = eigvecs.shape[-1]
    column_count = propagator.shape[-1]
    momentum_count = elementals.shape[1]
    vecs_flat = eigvecs.reshape(2, -1, vec_count)
    columns_both = jnp.concatenate([vecs_flat[0], vecs_flat[1]], axis=0)
    columns_swap = jnp.concatenate([-vecs_flat[1], vecs_flat[0]], axis=0)
    vec_both = jnp.stack([columns_both, columns_swap], axis=1)
    prop_cat = propagator.reshape(-1, column_count)
    moments = elementals[0]
    own_block = lax.psum_scatter(
        lax.dot_general(
            prop_cat, vec_both, (((0,), (0,)), ((), ())), preferred_element_type=jnp.float32
        ),
        "space",
        scatter_dimension=0,
        tiled=True,
    ).astype(jnp.bfloat16)
    expand = jnp.einsum("prab,sqb->prsqa", moments, own_block, preferred_element_type=jnp.float32)
    real_part = expand[:, 0, :, 0] - expand[:, 1, :, 1]
    imag_part = expand[:, 0, :, 1] + expand[:, 1, :, 0]
    mixed_terms = jnp.stack([real_part, imag_part], axis=2).astype(jnp.bfloat16)
    swapped = jnp.stack([mixed_terms[:, :, 1], -mixed_terms[:, :, 0]], axis=2)
    weights = jnp.stack([mixed_terms, swapped], axis=1).reshape(2 * momentum_count, -1)
    time_slots = lax.axis_size("tm")
    pick_mom = (momenta[0][:, None] == jnp.arange(momentum_count, dtype=jnp.int32)[None, :]).astype(
        jnp.float32
    )
    blocks = lax.all_gather(own_block[None], "tm", axis=0, tiled=True)
    flattened = blocks.reshape(blocks.shape[0], -1)
    tables = lax.dot_general(
        weights, flattened, (((1,), (1,)), ((), ())), preferred_element_type=jnp.float32
    )
    slot_index = sink_times[0]
    tables = tables.reshape(momentum_count, 2, time_slots)
    pick_time = (slot_index[:, None] == jnp.arange(time_slots, dtype=jnp.int32)[None, :]).astype(
        jnp.float32
    )
    spread = jnp.einsum("kp,pot->okt", pick_mom, tables, precision=lax.Precision.HIGHEST)
    picked = jnp.sum(spread * pick_time[None], axis=2)
    summed = lax.psum(picked, "space")
    return summed[:, None, :]


def solution(mesh):
    slice_count, space_count = mesh.shape["tm"], mesh.shape["space"]
    slice_bits, space_bits = slice_count.bit_length() - 1, space_count.bit_length() - 1
    on_device = by_collectives
    if (slice_count, space_count) == (1 << slice_bits, 1 << space_bits):
        if slice_bits > 2 and space_bits > 0 and space_bits % 2 == 0:
            on_device = functools.partial(by_exchanges, slice_count, space_count)
    return jax.shard_map(
        on_device,
        mesh=mesh,
        in_specs=(
            P(None, None, "tm", "space", None),
            P(None, None, "tm", "space", None),
            P("tm", None, None, None, None),
            P("tm", None),
            P("tm", None),
        ),
        out_specs=P(None, "tm", None),
        check_vma=False,
    )
```

```python
import functools

import jax
import jax.numpy as jnp
from jax import lax
from jax.experimental import pallas as pl
from jax.experimental.pallas import tpu as pltpu
from jax.sharding import PartitionSpec as P

MIB = 1 << 20


def project_kernel(vec_hbm, prop_hbm, keep_ref, send_ref, vec_buf, prop_buf, acc_ref, sems):
    colours = vec_buf.shape[1]
    vec_count = vec_buf.shape[-1]
    columns = prop_buf.shape[-1]
    half = columns // 2
    copies = []
    for c in range(colours):
        vec_copy = pltpu.make_async_copy(vec_hbm.at[:, c, 0], vec_buf.at[:, c], sems.at[0, c])
        prop_copy = pltpu.make_async_copy(prop_hbm.at[:, c, 0], prop_buf.at[:, c], sems.at[1, c])
        prop_copy.start()
        vec_copy.start()
        copies.append((vec_copy, prop_copy))
    for c in range(colours):
        for copy in copies[c]:
            copy.wait()
        lhs = jnp.concatenate([prop_buf[0, c], prop_buf[1, c]], axis=-1)
        rhs = jnp.concatenate([vec_buf[0, c], vec_buf[1, c]], axis=-1)
        part = lax.dot_general(
            lhs, rhs, (((0,), (0,)), ((), ())), preferred_element_type=jnp.float32
        )
        if c == 0:
            acc_ref[...] = part
        else:
            acc_ref[...] += part
    mine = lax.rem(lax.axis_index("space"), 2)
    for out_ref, which in ((send_ref, 1 - mine), (keep_ref, mine)):
        top = pl.ds(pl.multiple_of(which * half, half), half)
        low = pl.ds(pl.multiple_of(columns + which * half, half), half)
        real = acc_ref[top, :vec_count] + acc_ref[low, vec_count:]
        imag = acc_ref[low, :vec_count] - acc_ref[top, vec_count:]
        out_ref[0] = real.astype(out_ref.dtype)
        out_ref[1] = imag.astype(out_ref.dtype)


def project(eigvecs, propagator):
    _, colours, _, sites, vec_count = eigvecs.shape
    columns = propagator.shape[-1]
    shape = (2, columns // 2, vec_count)
    return pl.pallas_call(
        project_kernel,
        out_shape=(
            jax.ShapeDtypeStruct(shape, jnp.float32),
            jax.ShapeDtypeStruct(shape, jnp.bfloat16),
        ),
        in_specs=[pl.BlockSpec(memory_space=pl.ANY)] * 2,
        out_specs=[pl.BlockSpec(memory_space=pltpu.VMEM)] * 2,
        scratch_shapes=[
            pltpu.VMEM((2, colours, sites, vec_count), jnp.bfloat16),
            pltpu.VMEM((2, colours, sites, columns), jnp.bfloat16),
            pltpu.VMEM((2 * columns, 2 * vec_count), jnp.float32),
            pltpu.SemaphoreType.DMA((2, colours)),
        ],
        compiler_params=pltpu.CompilerParams(vmem_limit_bytes=107 * MIB // 2),
        name="project",
    )(eigvecs, propagator)


def mix_kernel(own_ref, other_ref, elem_ref, mixed_ref):
    momenta = elem_ref.shape[1]
    half = own_ref.shape[1]
    full = (own_ref[...] + other_ref[...]).astype(jnp.bfloat16)
    both = full.reshape(2 * half, full.shape[-1])
    for p in range(momenta):
        by_real, by_imag = (
            lax.dot_general(
                both, elem_ref[0, p, r], (((1,), (1,)), ((), ())), preferred_element_type=jnp.float32
            )
            for r in range(2)
        )
        mixed_ref[p, 0] = by_real[:half] - by_imag[half:]
        mixed_ref[p, 1] = by_imag[:half] + by_real[half:]


def mix(own, other, elementals):
    momenta = elementals.shape[1]
    size = own.size
    return pl.pallas_call(
        mix_kernel,
        out_shape=jax.ShapeDtypeStruct((momenta,) + own.shape, jnp.float32),
        in_specs=[pl.BlockSpec(memory_space=pltpu.VMEM)] * 3,
        out_specs=pl.BlockSpec(memory_space=pltpu.VMEM),
        compiler_params=pltpu.CompilerParams(vmem_limit_bytes=16 * MIB),
        cost_estimate=pl.CostEstimate(
            flops=4 * momenta * size * own.shape[-1], bytes_accessed=8 * size, transcendentals=0
        ),
        name="mix",
    )(own, other, elementals)


def trace_kernel(orders, sink_ref, mom_ref, mixed_ref, *refs):
    groups, out_ref, slices_ref, sums_ref = refs[:-3], refs[-3], refs[-2], refs[-1]
    items = out_ref.shape[1]
    per_group = groups[0].shape[0]
    own_slice = lax.axis_index("tm")
    own_core = own_slice & 1
    for g, ref in enumerate(groups):
        slices_ref[g * per_group : (g + 1) * per_group] = ref[...]
    for k in range(items):
        p = mom_ref[0, k]
        away = sink_ref[0, k] ^ own_slice
        crossed = away & 1
        slots = []
        for order in orders:
            slot = 0
            for place, bit in enumerate(order):
                slot = slot + (((away >> bit) & 1) << place)
            slots.append(slot)
        slot = jnp.where(own_core ^ crossed == 0, slots[0], slots[1])
        crossed = crossed ^ (slot >> (len(orders[0]) - 1))
        slot = slot + crossed * (2 * per_group)
        real = slices_ref[slot, 0].astype(jnp.float32)
        imag = slices_ref[slot, 1].astype(jnp.float32)
        mixed_real = mixed_ref[p, 0]
        mixed_imag = mixed_ref[p, 1]
        for o, value in enumerate(
            (mixed_real * real + mixed_imag * imag, mixed_imag * real - mixed_real * imag)
        ):
            rows, lanes = value.shape
            value = jnp.sum(value.reshape(rows // 8, 8, lanes), axis=0)
            sums_ref[o, k] = sum(value[:, i * 128 : (i + 1) * 128] for i in range(lanes // 128))
    out_ref[...] = jnp.sum(jnp.sum(sums_ref[...], axis=2), axis=-1)


def trace(orders, sink_times, momenta, mixed, groups):
    items = sink_times.shape[1]
    per_group = groups[0].shape[0]
    return pl.pallas_call(
        functools.partial(trace_kernel, orders),
        out_shape=jax.ShapeDtypeStruct((2, items), jnp.float32),
        in_specs=[pl.BlockSpec(memory_space=pltpu.VMEM)] * (3 + len(groups)),
        out_specs=pl.BlockSpec(memory_space=pltpu.VMEM),
        scratch_shapes=[
            pltpu.VMEM((len(groups) * per_group,) + groups[0].shape[1:], jnp.bfloat16),
            pltpu.VMEM((2, items, 8, 128), jnp.float32),
        ],
        compiler_params=pltpu.CompilerParams(vmem_limit_bytes=16 * MIB),
        name="trace",
    )(sink_times, momenta, mixed, *groups)


def by_exchanges(slice_count, space_count, eigvecs, propagator, elementals, sink_times, momenta):
    axes = ("tm", "space")
    slice_bits = slice_count.bit_length() - 1
    space_bits = space_count.bit_length() - 1
    orders = (tuple(range(1, slice_bits)), tuple(range(slice_bits - 1, 0, -1)))

    def exchange(value, partner):
        pairs = []
        for t in range(slice_count):
            for s in range(space_count):
                to_t, to_s = partner(t, s)
                pairs.append((t * space_count + s, to_t * space_count + to_s))
        return lax.ppermute(value, axes, pairs)

    def across(value, bit):
        return exchange(value, lambda t, s: (t, s ^ (1 << bit)))

    keep, send = project(eigvecs, propagator)
    own = keep + across(send, 0).astype(jnp.float32)
    blocks = own.astype(jnp.bfloat16)[None]
    total, other = own, jnp.zeros_like(own)
    for bit in range(1, space_bits):
        if bit > 1:
            total = total + other
        other = across(total, bit)
    for step in range(slice_bits - 1):
        flip = 1 if step == slice_bits - 2 else 0
        arrived = exchange(blocks, lambda t, s: (t ^ (1 << orders[t & 1][step]) ^ flip, s))
        if step < slice_bits - 2:
            blocks = jnp.concatenate([blocks, arrived], axis=0)
    arrived, other = lax.optimization_barrier((arrived, other))
    cross = lambda t, s: (t ^ 1, s)
    groups = [blocks, arrived, exchange(blocks, cross), exchange(arrived, cross)]
    mixed = mix(total, other, elementals)
    partial = trace(orders, sink_times, momenta, mixed, groups)
    for bit in range(space_bits):
        far = exchange(partial, lambda t, s: (t ^ 1, s ^ (1 << bit)))
        partial = far + exchange(partial, cross)
    return partial[:, None, :]


def by_collectives(eigvecs, propagator, elementals, sink_times, momenta):
    vec_count = eigvecs.shape[-1]
    column_count = propagator.shape[-1]
    momentum_count = elementals.shape[1]
    vecs_flat = eigvecs.reshape(2, -1, vec_count)
    columns_both = jnp.concatenate([vecs_flat[0], vecs_flat[1]], axis=0)
    columns_swap = jnp.concatenate([-vecs_flat[1], vecs_flat[0]], axis=0)
    vec_both = jnp.stack([columns_both, columns_swap], axis=1)
    prop_cat = propagator.reshape(-1, column_count)
    moments = elementals[0]
    own_block = lax.psum_scatter(
        lax.dot_general(
            prop_cat, vec_both, (((0,), (0,)), ((), ())), preferred_element_type=jnp.float32
        ),
        "space",
        scatter_dimension=0,
        tiled=True,
    ).astype(jnp.bfloat16)
    expand = jnp.einsum("prab,sqb->prsqa", moments, own_block, preferred_element_type=jnp.float32)
    real_part = expand[:, 0, :, 0] - expand[:, 1, :, 1]
    imag_part = expand[:, 0, :, 1] + expand[:, 1, :, 0]
    mixed_terms = jnp.stack([real_part, imag_part], axis=2).astype(jnp.bfloat16)
    swapped = jnp.stack([mixed_terms[:, :, 1], -mixed_terms[:, :, 0]], axis=2)
    weights = jnp.stack([mixed_terms, swapped], axis=1).reshape(2 * momentum_count, -1)
    time_slots = lax.axis_size("tm")
    pick_mom = (momenta[0][:, None] == jnp.arange(momentum_count, dtype=jnp.int32)[None, :]).astype(
        jnp.float32
    )
    blocks = lax.all_gather(own_block[None], "tm", axis=0, tiled=True)
    flattened = blocks.reshape(blocks.shape[0], -1)
    tables = lax.dot_general(
        weights, flattened, (((1,), (1,)), ((), ())), preferred_element_type=jnp.float32
    )
    slot_index = sink_times[0]
    tables = tables.reshape(momentum_count, 2, time_slots)
    pick_time = (slot_index[:, None] == jnp.arange(time_slots, dtype=jnp.int32)[None, :]).astype(
        jnp.float32
    )
    spread = jnp.einsum("kp,pot->okt", pick_mom, tables, precision=lax.Precision.HIGHEST)
    picked = jnp.sum(spread * pick_time[None], axis=2)
    summed = lax.psum(picked, "space")
    return summed[:, None, :]


def solution(mesh):
    slice_count, space_count = mesh.shape["tm"], mesh.shape["space"]
    slice_bits, space_bits = slice_count.bit_length() - 1, space_count.bit_length() - 1
    on_device = by_collectives
    if (slice_count, space_count) == (1 << slice_bits, 1 << space_bits):
        if slice_bits > 2 and space_bits > 0 and space_bits % 2 == 0:
            on_device = functools.partial(by_exchanges, slice_count, space_count)
    return jax.shard_map(
        on_device,
        mesh=mesh,
        in_specs=(
            P(None, None, "tm", "space", None),
            P(None, None, "tm", "space", None),
            P("tm", None, None, None, None),
            P("tm", None),
            P("tm", None),
        ),
        out_specs=P(None, "tm", None),
        check_vma=False,
    )
```

```python
import functools

import jax
import jax.numpy as jnp
from jax import lax
from jax.experimental import pallas as pl
from jax.experimental.pallas import tpu as pltpu
from jax.sharding import PartitionSpec as P

MIB = 1 << 20


def project_kernel(vec_hbm, prop_hbm, keep_ref, send_ref, vec_buf, prop_buf, acc_ref, sems):
    colours = vec_buf.shape[1]
    vec_count = vec_buf.shape[-1]
    columns = prop_buf.shape[-1]
    half = columns // 2
    copies = []
    for c in range(colours):
        vec_copy = pltpu.make_async_copy(vec_hbm.at[:, c, 0], vec_buf.at[:, c], sems.at[0, c])
        prop_copy = pltpu.make_async_copy(prop_hbm.at[:, c, 0], prop_buf.at[:, c], sems.at[1, c])
        prop_copy.start()
        vec_copy.start()
        copies.append((vec_copy, prop_copy))
    for c in range(colours):
        for copy in copies[c]:
            copy.wait()
        lhs = jnp.concatenate([prop_buf[0, c], prop_buf[1, c]], axis=-1)
        rhs = jnp.concatenate([vec_buf[0, c], vec_buf[1, c]], axis=-1)
        part = lax.dot_general(
            lhs, rhs, (((0,), (0,)), ((), ())), preferred_element_type=jnp.float32
        )
        if c == 0:
            acc_ref[...] = part
        else:
            acc_ref[...] += part
    mine = lax.rem(lax.axis_index("space"), 2)
    for out_ref, which in ((send_ref, 1 - mine), (keep_ref, mine)):
        top = pl.ds(pl.multiple_of(which * half, half), half)
        low = pl.ds(pl.multiple_of(columns + which * half, half), half)
        real = acc_ref[top, :vec_count] + acc_ref[low, vec_count:]
        imag = acc_ref[low, :vec_count] - acc_ref[top, vec_count:]
        out_ref[0] = real.astype(out_ref.dtype)
        out_ref[1] = imag.astype(out_ref.dtype)


def project(eigvecs, propagator):
    _, colours, _, sites, vec_count = eigvecs.shape
    columns = propagator.shape[-1]
    shape = (2, columns // 2, vec_count)
    return pl.pallas_call(
        project_kernel,
        out_shape=(
            jax.ShapeDtypeStruct(shape, jnp.float32),
            jax.ShapeDtypeStruct(shape, jnp.bfloat16),
        ),
        in_specs=[pl.BlockSpec(memory_space=pl.ANY)] * 2,
        out_specs=[pl.BlockSpec(memory_space=pltpu.VMEM)] * 2,
        scratch_shapes=[
            pltpu.VMEM((2, colours, sites, vec_count), jnp.bfloat16),
            pltpu.VMEM((2, colours, sites, columns), jnp.bfloat16),
            pltpu.VMEM((2 * columns, 2 * vec_count), jnp.float32),
            pltpu.SemaphoreType.DMA((2, colours)),
        ],
        compiler_params=pltpu.CompilerParams(vmem_limit_bytes=107 * MIB // 2),
        name="project",
    )(eigvecs, propagator)


def mix_kernel(own_ref, other_ref, elem_ref, mixed_ref):
    momenta = elem_ref.shape[1]
    half = own_ref.shape[1]
    full = own_ref[...] + other_ref[...].astype(jnp.float32)
    full = full.reshape(2 * half, full.shape[-1])
    high = full.astype(jnp.bfloat16)
    low = (full - high.astype(jnp.float32)).astype(jnp.bfloat16)
    both = jnp.concatenate([high, low], axis=0)
    for p in range(momenta):
        by_real, by_imag = (
            lax.dot_general(
                both, elem_ref[0, p, r], (((1,), (1,)), ((), ())), preferred_element_type=jnp.float32
            )
            for r in range(2)
        )
        by_real = by_real[: 2 * half] + by_real[2 * half :]
        by_imag = by_imag[: 2 * half] + by_imag[2 * half :]
        mixed_ref[p, 0] = by_real[:half] - by_imag[half:]
        mixed_ref[p, 1] = by_imag[:half] + by_real[half:]


def mix(own, other, elementals):
    momenta = elementals.shape[1]
    size = own.size
    return pl.pallas_call(
        mix_kernel,
        out_shape=jax.ShapeDtypeStruct((momenta,) + own.shape, jnp.float32),
        in_specs=[pl.BlockSpec(memory_space=pltpu.VMEM)] * 3,
        out_specs=pl.BlockSpec(memory_space=pltpu.VMEM),
        compiler_params=pltpu.CompilerParams(vmem_limit_bytes=16 * MIB),
        cost_estimate=pl.CostEstimate(
            flops=4 * momenta * size * own.shape[-1], bytes_accessed=8 * size, transcendentals=0
        ),
        name="mix",
    )(own, other, elementals)


def trace_kernel(orders, sink_ref, mom_ref, mixed_ref, *refs):
    groups, out_ref, slices_ref, sums_ref = refs[:-3], refs[-3], refs[-2], refs[-1]
    items = out_ref.shape[1]
    per_group = groups[0].shape[0]
    own_slice = lax.axis_index("tm")
    own_core = own_slice & 1
    for g, ref in enumerate(groups):
        slices_ref[g * per_group : (g + 1) * per_group] = ref[...]
    for k in range(items):
        p = mom_ref[0, k]
        away = sink_ref[0, k] ^ own_slice
        crossed = away & 1
        slots = []
        for order in orders:
            slot = 0
            for place, bit in enumerate(order):
                slot = slot + (((away >> bit) & 1) << place)
            slots.append(slot)
        slot = jnp.where(own_core ^ crossed == 0, slots[0], slots[1])
        crossed = crossed ^ (slot >> (len(orders[0]) - 1))
        slot = slot + crossed * (2 * per_group)
        real = slices_ref[slot, 0].astype(jnp.float32)
        imag = slices_ref[slot, 1].astype(jnp.float32)
        mixed_real = mixed_ref[p, 0]
        mixed_imag = mixed_ref[p, 1]
        for o, value in enumerate(
            (mixed_real * real + mixed_imag * imag, mixed_imag * real - mixed_real * imag)
        ):
            rows, lanes = value.shape
            value = jnp.sum(value.reshape(rows // 8, 8, lanes), axis=0)
            sums_ref[o, k] = sum(value[:, i * 128 : (i + 1) * 128] for i in range(lanes // 128))
    out_ref[...] = jnp.sum(jnp.sum(sums_ref[...], axis=2), axis=-1)


def trace(orders, sink_times, momenta, mixed, groups):
    items = sink_times.shape[1]
    per_group = groups[0].shape[0]
    return pl.pallas_call(
        functools.partial(trace_kernel, orders),
        out_shape=jax.ShapeDtypeStruct((2, items), jnp.float32),
        in_specs=[pl.BlockSpec(memory_space=pltpu.VMEM)] * (3 + len(groups)),
        out_specs=pl.BlockSpec(memory_space=pltpu.VMEM),
        scratch_shapes=[
            pltpu.VMEM((len(groups) * per_group,) + groups[0].shape[1:], jnp.bfloat16),
            pltpu.VMEM((2, items, 8, 128), jnp.float32),
        ],
        compiler_params=pltpu.CompilerParams(vmem_limit_bytes=16 * MIB),
        name="trace",
    )(sink_times, momenta, mixed, *groups)


def by_exchanges(slice_count, space_count, eigvecs, propagator, elementals, sink_times, momenta):
    axes = ("tm", "space")
    slice_bits = slice_count.bit_length() - 1
    space_bits = space_count.bit_length() - 1
    orders = (tuple(range(1, slice_bits)), tuple(range(slice_bits - 1, 0, -1)))

    def exchange(value, partner):
        pairs = []
        for t in range(slice_count):
            for s in range(space_count):
                to_t, to_s = partner(t, s)
                pairs.append((t * space_count + s, to_t * space_count + to_s))
        return lax.ppermute(value, axes, pairs)

    def across(value, bit):
        return exchange(value, lambda t, s: (t, s ^ (1 << bit)))

    keep, send = project(eigvecs, propagator)
    own = keep + across(send, 0).astype(jnp.float32)
    blocks = own.astype(jnp.bfloat16)[None]
    other = across(blocks[0], 1)
    for step in range(slice_bits - 1):
        flip = 1 if step == slice_bits - 2 else 0
        arrived = exchange(blocks, lambda t, s: (t ^ (1 << orders[t & 1][step]) ^ flip, s))
        if step < slice_bits - 2:
            blocks = jnp.concatenate([blocks, arrived], axis=0)
    cross = lambda t, s: (t ^ 1, s)
    blocks_late, other = lax.optimization_barrier((blocks, other))
    swapped = exchange(blocks_late, cross)
    arrived, swapped = lax.optimization_barrier((arrived, swapped))
    groups = [blocks, arrived, swapped, exchange(arrived, cross)]
    mixed = mix(own, other, elementals)
    partial = trace(orders, sink_times, momenta, mixed, groups)
    for bit in range(space_bits):
        far = exchange(partial, lambda t, s: (t ^ 1, s ^ (1 << bit)))
        partial = far + exchange(partial, cross)
    return partial[:, None, :]


def by_collectives(eigvecs, propagator, elementals, sink_times, momenta):
    vec_count = eigvecs.shape[-1]
    column_count = propagator.shape[-1]
    momentum_count = elementals.shape[1]
    vecs_flat = eigvecs.reshape(2, -1, vec_count)
    columns_both = jnp.concatenate([vecs_flat[0], vecs_flat[1]], axis=0)
    columns_swap = jnp.concatenate([-vecs_flat[1], vecs_flat[0]], axis=0)
    vec_both = jnp.stack([columns_both, columns_swap], axis=1)
    prop_cat = propagator.reshape(-1, column_count)
    moments = elementals[0]
    own_block = lax.psum_scatter(
        lax.dot_general(
            prop_cat, vec_both, (((0,), (0,)), ((), ())), preferred_element_type=jnp.float32
        ),
        "space",
        scatter_dimension=0,
        tiled=True,
    ).astype(jnp.bfloat16)
    expand = jnp.einsum("prab,sqb->prsqa", moments, own_block, preferred_element_type=jnp.float32)
    real_part = expand[:, 0, :, 0] - expand[:, 1, :, 1]
    imag_part = expand[:, 0, :, 1] + expand[:, 1, :, 0]
    mixed_terms = jnp.stack([real_part, imag_part], axis=2).astype(jnp.bfloat16)
    swapped = jnp.stack([mixed_terms[:, :, 1], -mixed_terms[:, :, 0]], axis=2)
    weights = jnp.stack([mixed_terms, swapped], axis=1).reshape(2 * momentum_count, -1)
    time_slots = lax.axis_size("tm")
    pick_mom = (momenta[0][:, None] == jnp.arange(momentum_count, dtype=jnp.int32)[None, :]).astype(
        jnp.float32
    )
    blocks = lax.all_gather(own_block[None], "tm", axis=0, tiled=True)
    flattened = blocks.reshape(blocks.shape[0], -1)
    tables = lax.dot_general(
        weights, flattened, (((1,), (1,)), ((), ())), preferred_element_type=jnp.float32
    )
    slot_index = sink_times[0]
    tables = tables.reshape(momentum_count, 2, time_slots)
    pick_time = (slot_index[:, None] == jnp.arange(time_slots, dtype=jnp.int32)[None, :]).astype(
        jnp.float32
    )
    spread = jnp.einsum("kp,pot->okt", pick_mom, tables, precision=lax.Precision.HIGHEST)
    picked = jnp.sum(spread * pick_time[None], axis=2)
    summed = lax.psum(picked, "space")
    return summed[:, None, :]


def solution(mesh):
    slice_count, space_count = mesh.shape["tm"], mesh.shape["space"]
    slice_bits, space_bits = slice_count.bit_length() - 1, space_count.bit_length() - 1
    on_device = by_collectives
    if (slice_count, space_count) == (1 << slice_bits, 1 << space_bits):
        if slice_bits > 2 and space_bits == 2:
            on_device = functools.partial(by_exchanges, slice_count, space_count)
    return jax.shard_map(
        on_device,
        mesh=mesh,
        in_specs=(
            P(None, None, "tm", "space", None),
            P(None, None, "tm", "space", None),
            P("tm", None, None, None, None),
            P("tm", None),
            P("tm", None),
        ),
        out_specs=P(None, "tm", None),
        check_vma=False,
    )
```

```python
import functools

import jax
import jax.numpy as jnp
from jax import lax
from jax.experimental import pallas as pl
from jax.experimental.pallas import tpu as pltpu
from jax.sharding import PartitionSpec as P

MIB = 1 << 20


def project_kernel(vec_hbm, prop_hbm, keep_ref, send_ref, vec_buf, prop_buf, acc_ref, sems):
    colours = vec_buf.shape[1]
    vec_count = vec_buf.shape[-1]
    columns = prop_buf.shape[-1]
    half = columns // 2
    copies = []
    for c in range(colours):
        vec_copy = pltpu.make_async_copy(vec_hbm.at[:, c, 0], vec_buf.at[:, c], sems.at[0, c])
        prop_copy = pltpu.make_async_copy(prop_hbm.at[:, c, 0], prop_buf.at[:, c], sems.at[1, c])
        prop_copy.start()
        vec_copy.start()
        copies.append((vec_copy, prop_copy))
    for c in range(colours):
        for copy in copies[c]:
            copy.wait()
        lhs = jnp.concatenate([prop_buf[0, c], prop_buf[1, c]], axis=-1)
        rhs = jnp.concatenate([vec_buf[0, c], vec_buf[1, c]], axis=-1)
        part = lax.dot_general(
            lhs, rhs, (((0,), (0,)), ((), ())), preferred_element_type=jnp.float32
        )
        if c == 0:
            acc_ref[...] = part
        else:
            acc_ref[...] += part
    mine = lax.rem(lax.axis_index("space"), 2)
    for out_ref, which in ((send_ref, 1 - mine), (keep_ref, mine)):
        top = pl.ds(pl.multiple_of(which * half, half), half)
        low = pl.ds(pl.multiple_of(columns + which * half, half), half)
        real = acc_ref[top, :vec_count] + acc_ref[low, vec_count:]
        imag = acc_ref[low, :vec_count] - acc_ref[top, vec_count:]
        out_ref[0] = real.astype(out_ref.dtype)
        out_ref[1] = imag.astype(out_ref.dtype)


def project(eigvecs, propagator):
    _, colours, _, sites, vec_count = eigvecs.shape
    columns = propagator.shape[-1]
    shape = (2, columns // 2, vec_count)
    return pl.pallas_call(
        project_kernel,
        out_shape=(
            jax.ShapeDtypeStruct(shape, jnp.float32),
            jax.ShapeDtypeStruct(shape, jnp.bfloat16),
        ),
        in_specs=[pl.BlockSpec(memory_space=pl.ANY)] * 2,
        out_specs=[pl.BlockSpec(memory_space=pltpu.VMEM)] * 2,
        scratch_shapes=[
            pltpu.VMEM((2, colours, sites, vec_count), jnp.bfloat16),
            pltpu.VMEM((2, colours, sites, columns), jnp.bfloat16),
            pltpu.VMEM((2 * columns, 2 * vec_count), jnp.float32),
            pltpu.SemaphoreType.DMA((2, colours)),
        ],
        compiler_params=pltpu.CompilerParams(vmem_limit_bytes=107 * MIB // 2),
        name="project",
    )(eigvecs, propagator)


def mix_kernel(own_ref, other_ref, elem_ref, mixed_ref):
    momenta = elem_ref.shape[1]
    half = own_ref.shape[1]
    full = own_ref[...] + other_ref[...].astype(jnp.float32)
    full = full.reshape(2 * half, full.shape[-1])
    high = full.astype(jnp.bfloat16)
    low = (full - high.astype(jnp.float32)).astype(jnp.bfloat16)
    both = jnp.concatenate([high, low], axis=0)
    for p in range(momenta):
        by_real, by_imag = (
            lax.dot_general(
                both, elem_ref[0, p, r], (((1,), (1,)), ((), ())), preferred_element_type=jnp.float32
            )
            for r in range(2)
        )
        by_real = by_real[: 2 * half] + by_real[2 * half :]
        by_imag = by_imag[: 2 * half] + by_imag[2 * half :]
        mixed_ref[p, 0] = by_real[:half] - by_imag[half:]
        mixed_ref[p, 1] = by_imag[:half] + by_real[half:]


def mix(own, other, elementals):
    momenta = elementals.shape[1]
    size = own.size
    return pl.pallas_call(
        mix_kernel,
        out_shape=jax.ShapeDtypeStruct((momenta,) + own.shape, jnp.float32),
        in_specs=[pl.BlockSpec(memory_space=pltpu.VMEM)] * 3,
        out_specs=pl.BlockSpec(memory_space=pltpu.VMEM),
        compiler_params=pltpu.CompilerParams(vmem_limit_bytes=16 * MIB),
        cost_estimate=pl.CostEstimate(
            flops=4 * momenta * size * own.shape[-1], bytes_accessed=8 * size, transcendentals=0
        ),
        name="mix",
    )(own, other, elementals)


def trace_kernel(slot_ref, mom_ref, mixed_ref, *refs):
    groups, out_ref, slices_ref, sums_ref = refs[:-3], refs[-3], refs[-2], refs[-1]
    items = out_ref.shape[1]
    for g, ref in enumerate(groups):
        slices_ref[g * ref.shape[0] : (g + 1) * ref.shape[0]] = ref[...]
    for k in range(items):
        p = mom_ref[0, k]
        slot = slot_ref[0, k]
        real = slices_ref[slot, 0].astype(jnp.float32)
        imag = slices_ref[slot, 1].astype(jnp.float32)
        mixed_real = mixed_ref[p, 0]
        mixed_imag = mixed_ref[p, 1]
        for o, value in enumerate(
            (mixed_real * real + mixed_imag * imag, mixed_imag * real - mixed_real * imag)
        ):
            rows, lanes = value.shape
            value = jnp.sum(value.reshape(rows // 8, 8, lanes), axis=0)
            sums_ref[o, k] = sum(value[:, i * 128 : (i + 1) * 128] for i in range(lanes // 128))
    out_ref[...] = jnp.sum(jnp.sum(sums_ref[...], axis=2), axis=-1)


def trace(slots, momenta, mixed, groups):
    items = slots.shape[1]
    per_group = groups[0].shape[0]
    return pl.pallas_call(
        trace_kernel,
        out_shape=jax.ShapeDtypeStruct((2, items), jnp.float32),
        in_specs=[pl.BlockSpec(memory_space=pltpu.VMEM)] * (3 + len(groups)),
        out_specs=pl.BlockSpec(memory_space=pltpu.VMEM),
        scratch_shapes=[
            pltpu.VMEM((len(groups) * per_group,) + groups[0].shape[1:], jnp.bfloat16),
            pltpu.VMEM((2, items, 8, 128), jnp.float32),
        ],
        compiler_params=pltpu.CompilerParams(vmem_limit_bytes=16 * MIB),
        name="trace",
    )(slots, momenta, mixed, *groups)


def slots_of(orders, sink_times):
    own_slice = lax.axis_index("tm")
    steps = len(orders[0])
    away = sink_times ^ own_slice
    by_core = []
    for order in orders:
        slot = jnp.zeros_like(away)
        for place, bit in enumerate(order):
            slot = slot + (((away >> bit) & 1) << place)
        by_core.append(slot)
    slot = jnp.where(sink_times & 1 == 0, by_core[0], by_core[1])
    crossed = (away & 1) ^ (slot >> (steps - 1))
    return slot + (crossed << steps)


def by_exchanges(slice_count, space_count, eigvecs, propagator, elementals, sink_times, momenta):
    axes = ("tm", "space")
    slice_bits = slice_count.bit_length() - 1
    space_bits = space_count.bit_length() - 1
    orders = (tuple(range(1, slice_bits)), tuple(range(slice_bits - 1, 0, -1)))

    def exchange(value, partner):
        pairs = []
        for t in range(slice_count):
            for s in range(space_count):
                to_t, to_s = partner(t, s)
                pairs.append((t * space_count + s, to_t * space_count + to_s))
        return lax.ppermute(value, axes, pairs)

    def across(value, bit):
        return exchange(value, lambda t, s: (t, s ^ (1 << bit)))

    keep, send = project(eigvecs, propagator)
    own = keep + across(send, 0).astype(jnp.float32)
    blocks = own.astype(jnp.bfloat16)[None]
    other = across(blocks[0], 1)
    for step in range(slice_bits - 1):
        flip = 1 if step == slice_bits - 2 else 0
        arrived = exchange(blocks, lambda t, s: (t ^ (1 << orders[t & 1][step]) ^ flip, s))
        if step < slice_bits - 2:
            blocks = jnp.concatenate([blocks, arrived], axis=0)
    cross = lambda t, s: (t ^ 1, s)
    blocks_late, other = lax.optimization_barrier((blocks, other))
    swapped = exchange(blocks_late, cross)
    arrived, swapped = lax.optimization_barrier((arrived, swapped))
    groups = [blocks, arrived, swapped, exchange(arrived, cross)]
    mixed = mix(own, other, elementals)
    partial = trace(slots_of(orders, sink_times), momenta, mixed, groups)
    for bit in range(space_bits):
        far = exchange(partial, lambda t, s: (t ^ 1, s ^ (1 << bit)))
        partial = far + exchange(partial, cross)
    return partial[:, None, :]


def by_collectives(eigvecs, propagator, elementals, sink_times, momenta):
    vec_count = eigvecs.shape[-1]
    column_count = propagator.shape[-1]
    momentum_count = elementals.shape[1]
    vecs_flat = eigvecs.reshape(2, -1, vec_count)
    columns_both = jnp.concatenate([vecs_flat[0], vecs_flat[1]], axis=0)
    columns_swap = jnp.concatenate([-vecs_flat[1], vecs_flat[0]], axis=0)
    vec_both = jnp.stack([columns_both, columns_swap], axis=1)
    prop_cat = propagator.reshape(-1, column_count)
    moments = elementals[0]
    own_block = lax.psum_scatter(
        lax.dot_general(
            prop_cat, vec_both, (((0,), (0,)), ((), ())), preferred_element_type=jnp.float32
        ),
        "space",
        scatter_dimension=0,
        tiled=True,
    ).astype(jnp.bfloat16)
    expand = jnp.einsum("prab,sqb->prsqa", moments, own_block, preferred_element_type=jnp.float32)
    real_part = expand[:, 0, :, 0] - expand[:, 1, :, 1]
    imag_part = expand[:, 0, :, 1] + expand[:, 1, :, 0]
    mixed_terms = jnp.stack([real_part, imag_part], axis=2).astype(jnp.bfloat16)
    swapped = jnp.stack([mixed_terms[:, :, 1], -mixed_terms[:, :, 0]], axis=2)
    weights = jnp.stack([mixed_terms, swapped], axis=1).reshape(2 * momentum_count, -1)
    time_slots = lax.axis_size("tm")
    pick_mom = (momenta[0][:, None] == jnp.arange(momentum_count, dtype=jnp.int32)[None, :]).astype(
        jnp.float32
    )
    blocks = lax.all_gather(own_block[None], "tm", axis=0, tiled=True)
    flattened = blocks.reshape(blocks.shape[0], -1)
    tables = lax.dot_general(
        weights, flattened, (((1,), (1,)), ((), ())), preferred_element_type=jnp.float32
    )
    slot_index = sink_times[0]
    tables = tables.reshape(momentum_count, 2, time_slots)
    pick_time = (slot_index[:, None] == jnp.arange(time_slots, dtype=jnp.int32)[None, :]).astype(
        jnp.float32
    )
    spread = jnp.einsum("kp,pot->okt", pick_mom, tables, precision=lax.Precision.HIGHEST)
    picked = jnp.sum(spread * pick_time[None], axis=2)
    summed = lax.psum(picked, "space")
    return summed[:, None, :]


def solution(mesh):
    slice_count, space_count = mesh.shape["tm"], mesh.shape["space"]
    slice_bits, space_bits = slice_count.bit_length() - 1, space_count.bit_length() - 1
    on_device = by_collectives
    if (slice_count, space_count) == (1 << slice_bits, 1 << space_bits):
        if slice_bits > 2 and space_bits == 2:
            on_device = functools.partial(by_exchanges, slice_count, space_count)
    return jax.shard_map(
        on_device,
        mesh=mesh,
        in_specs=(
            P(None, None, "tm", "space", None),
            P(None, None, "tm", "space", None),
            P("tm", None, None, None, None),
            P("tm", None),
            P("tm", None),
        ),
        out_specs=P(None, "tm", None),
        check_vma=False,
    )
```

```python
import functools

import jax
import jax.numpy as jnp
from jax import lax
from jax.experimental import pallas as pl
from jax.experimental.pallas import tpu as pltpu
from jax.sharding import PartitionSpec as P

MIB = 1 << 20


def project_kernel(vec_hbm, prop_hbm, keep_ref, send_ref, vec_buf, prop_buf, acc_ref, sems):
    colours = vec_buf.shape[1]
    vec_count = vec_buf.shape[-1]
    columns = prop_buf.shape[-1]
    half = columns // 2
    copies = []
    for c in range(colours):
        vec_copy = pltpu.make_async_copy(vec_hbm.at[:, c, 0], vec_buf.at[:, c], sems.at[0, c])
        prop_copy = pltpu.make_async_copy(prop_hbm.at[:, c, 0], prop_buf.at[:, c], sems.at[1, c])
        prop_copy.start()
        vec_copy.start()
        copies.append((vec_copy, prop_copy))
    for c in range(colours):
        for copy in copies[c]:
            copy.wait()
        lhs = jnp.concatenate([prop_buf[0, c], prop_buf[1, c]], axis=-1)
        rhs = jnp.concatenate([vec_buf[0, c], vec_buf[1, c]], axis=-1)
        part = lax.dot_general(
            lhs, rhs, (((0,), (0,)), ((), ())), preferred_element_type=jnp.float32
        )
        if c == 0:
            acc_ref[...] = part
        else:
            acc_ref[...] += part
    mine = lax.rem(lax.axis_index("space"), 2)
    for out_ref, which in ((send_ref, 1 - mine), (keep_ref, mine)):
        top = pl.ds(pl.multiple_of(which * half, half), half)
        low = pl.ds(pl.multiple_of(columns + which * half, half), half)
        real = acc_ref[top, :vec_count] + acc_ref[low, vec_count:]
        imag = acc_ref[low, :vec_count] - acc_ref[top, vec_count:]
        out_ref[0] = real.astype(out_ref.dtype)
        out_ref[1] = imag.astype(out_ref.dtype)


def project(eigvecs, propagator):
    _, colours, _, sites, vec_count = eigvecs.shape
    columns = propagator.shape[-1]
    shape = (2, columns // 2, vec_count)
    return pl.pallas_call(
        project_kernel,
        out_shape=(
            jax.ShapeDtypeStruct(shape, jnp.float32),
            jax.ShapeDtypeStruct(shape, jnp.bfloat16),
        ),
        in_specs=[pl.BlockSpec(memory_space=pl.ANY)] * 2,
        out_specs=[pl.BlockSpec(memory_space=pltpu.VMEM)] * 2,
        scratch_shapes=[
            pltpu.VMEM((2, colours, sites, vec_count), jnp.bfloat16),
            pltpu.VMEM((2, colours, sites, columns), jnp.bfloat16),
            pltpu.VMEM((2 * columns, 2 * vec_count), jnp.float32),
            pltpu.SemaphoreType.DMA((2, colours)),
        ],
        compiler_params=pltpu.CompilerParams(vmem_limit_bytes=107 * MIB // 2),
        name="project",
    )(eigvecs, propagator)


def mix_kernel(own_ref, other_ref, elem_ref, mixed_ref):
    momenta = elem_ref.shape[1]
    half = own_ref.shape[1]
    full = own_ref[...] + other_ref[...].astype(jnp.float32)
    full = full.reshape(2 * half, full.shape[-1])
    high = full.astype(jnp.bfloat16)
    low = (full - high.astype(jnp.float32)).astype(jnp.bfloat16)
    both = jnp.concatenate([high, low], axis=0)
    for p in range(momenta):
        by_real, by_imag = (
            lax.dot_general(
                both, elem_ref[0, p, r], (((1,), (1,)), ((), ())), preferred_element_type=jnp.float32
            )
            for r in range(2)
        )
        by_real = by_real[: 2 * half] + by_real[2 * half :]
        by_imag = by_imag[: 2 * half] + by_imag[2 * half :]
        mixed_ref[p, 0] = by_real[:half] - by_imag[half:]
        mixed_ref[p, 1] = by_imag[:half] + by_real[half:]


def mix(own, other, elementals):
    momenta = elementals.shape[1]
    size = own.size
    return pl.pallas_call(
        mix_kernel,
        out_shape=jax.ShapeDtypeStruct((momenta,) + own.shape, jnp.float32),
        in_specs=[pl.BlockSpec(memory_space=pltpu.VMEM)] * 3,
        out_specs=pl.BlockSpec(memory_space=pltpu.VMEM),
        compiler_params=pltpu.CompilerParams(vmem_limit_bytes=16 * MIB),
        cost_estimate=pl.CostEstimate(
            flops=4 * momenta * size * own.shape[-1], bytes_accessed=8 * size, transcendentals=0
        ),
        name="mix",
    )(own, other, elementals)


def trace_kernel(slot_ref, mom_ref, mixed_ref, *refs):
    groups, out_ref, slices_ref, sums_ref = refs[:-3], refs[-3], refs[-2], refs[-1]
    items = out_ref.shape[1]
    for g, ref in enumerate(groups):
        slices_ref[g * ref.shape[0] : (g + 1) * ref.shape[0]] = ref[...]
    for k in range(items):
        p = mom_ref[0, k]
        slot = slot_ref[0, k]
        real = slices_ref[slot, 0].astype(jnp.float32)
        imag = slices_ref[slot, 1].astype(jnp.float32)
        mixed_real = mixed_ref[p, 0]
        mixed_imag = mixed_ref[p, 1]
        for o, value in enumerate(
            (mixed_real * real + mixed_imag * imag, mixed_imag * real - mixed_real * imag)
        ):
            rows, lanes = value.shape
            value = jnp.sum(value.reshape(rows // 8, 8, lanes), axis=0)
            sums_ref[o, k] = sum(value[:, i * 128 : (i + 1) * 128] for i in range(lanes // 128))
    out_ref[...] = jnp.sum(jnp.sum(sums_ref[...], axis=2), axis=-1)


def trace(slots, momenta, mixed, groups):
    items = slots.shape[1]
    per_group = groups[0].shape[0]
    return pl.pallas_call(
        trace_kernel,
        out_shape=jax.ShapeDtypeStruct((2, items), jnp.float32),
        in_specs=[pl.BlockSpec(memory_space=pltpu.VMEM)] * (3 + len(groups)),
        out_specs=pl.BlockSpec(memory_space=pltpu.VMEM),
        scratch_shapes=[
            pltpu.VMEM((len(groups) * per_group,) + groups[0].shape[1:], jnp.bfloat16),
            pltpu.VMEM((2, items, 8, 128), jnp.float32),
        ],
        compiler_params=pltpu.CompilerParams(vmem_limit_bytes=16 * MIB),
        name="trace",
    )(slots, momenta, mixed, *groups)


def slots_of(orders, sink_times):
    own_slice = lax.axis_index("tm")
    steps = len(orders[0])
    away = sink_times ^ own_slice
    by_core = []
    for order in orders:
        slot = jnp.zeros_like(away)
        for place, bit in enumerate(order):
            slot = slot + (((away >> bit) & 1) << place)
        by_core.append(slot)
    slot = jnp.where(sink_times & 1 == 0, by_core[0], by_core[1])
    crossed = (away & 1) ^ (slot >> (steps - 1))
    return slot + (crossed << steps)


def by_exchanges(slice_count, space_count, eigvecs, propagator, elementals, sink_times, momenta):
    axes = ("tm", "space")
    slice_bits = slice_count.bit_length() - 1
    space_bits = space_count.bit_length() - 1
    orders = (tuple(range(1, slice_bits)), tuple(range(slice_bits - 1, 0, -1)))

    def exchange(value, partner):
        pairs = []
        for t in range(slice_count):
            for s in range(space_count):
                to_t, to_s = partner(t, s)
                pairs.append((t * space_count + s, to_t * space_count + to_s))
        return lax.ppermute(value, axes, pairs)

    def across(value, bit):
        return exchange(value, lambda t, s: (t, s ^ (1 << bit)))

    keep, send = project(eigvecs, propagator)
    own = keep + across(send, 0).astype(jnp.float32)
    blocks = own.astype(jnp.bfloat16)[None]
    other = across(blocks[0], 1)
    for step in range(slice_bits - 1):
        flip = 1 if step == slice_bits - 2 else 0
        arrived = exchange(blocks, lambda t, s: (t ^ (1 << orders[t & 1][step]) ^ flip, s))
        if step < slice_bits - 2:
            blocks = jnp.concatenate([blocks, arrived], axis=0)
    cross = lambda t, s: (t ^ 1, s)
    blocks_late, other = lax.optimization_barrier((blocks, other))
    swapped = exchange(blocks_late, cross)
    arrived, swapped = lax.optimization_barrier((arrived, swapped))
    groups = [blocks, arrived, swapped, exchange(arrived, cross)]
    mixed = mix(own, other, elementals)
    partial = trace(slots_of(orders, sink_times), momenta, mixed, groups)
    for bit in reversed(range(space_bits)):
        far = exchange(partial, lambda t, s: (t ^ 1, s ^ (1 << bit)))
        partial = far + exchange(partial, cross)
    return partial[:, None, :]


def by_collectives(eigvecs, propagator, elementals, sink_times, momenta):
    vec_count = eigvecs.shape[-1]
    column_count = propagator.shape[-1]
    momentum_count = elementals.shape[1]
    vecs_flat = eigvecs.reshape(2, -1, vec_count)
    columns_both = jnp.concatenate([vecs_flat[0], vecs_flat[1]], axis=0)
    columns_swap = jnp.concatenate([-vecs_flat[1], vecs_flat[0]], axis=0)
    vec_both = jnp.stack([columns_both, columns_swap], axis=1)
    prop_cat = propagator.reshape(-1, column_count)
    moments = elementals[0]
    own_block = lax.psum_scatter(
        lax.dot_general(
            prop_cat, vec_both, (((0,), (0,)), ((), ())), preferred_element_type=jnp.float32
        ),
        "space",
        scatter_dimension=0,
        tiled=True,
    ).astype(jnp.bfloat16)
    expand = jnp.einsum("prab,sqb->prsqa", moments, own_block, preferred_element_type=jnp.float32)
    real_part = expand[:, 0, :, 0] - expand[:, 1, :, 1]
    imag_part = expand[:, 0, :, 1] + expand[:, 1, :, 0]
    mixed_terms = jnp.stack([real_part, imag_part], axis=2).astype(jnp.bfloat16)
    swapped = jnp.stack([mixed_terms[:, :, 1], -mixed_terms[:, :, 0]], axis=2)
    weights = jnp.stack([mixed_terms, swapped], axis=1).reshape(2 * momentum_count, -1)
    time_slots = lax.axis_size("tm")
    pick_mom = (momenta[0][:, None] == jnp.arange(momentum_count, dtype=jnp.int32)[None, :]).astype(
        jnp.float32
    )
    blocks = lax.all_gather(own_block[None], "tm", axis=0, tiled=True)
    flattened = blocks.reshape(blocks.shape[0], -1)
    tables = lax.dot_general(
        weights, flattened, (((1,), (1,)), ((), ())), preferred_element_type=jnp.float32
    )
    slot_index = sink_times[0]
    tables = tables.reshape(momentum_count, 2, time_slots)
    pick_time = (slot_index[:, None] == jnp.arange(time_slots, dtype=jnp.int32)[None, :]).astype(
        jnp.float32
    )
    spread = jnp.einsum("kp,pot->okt", pick_mom, tables, precision=lax.Precision.HIGHEST)
    picked = jnp.sum(spread * pick_time[None], axis=2)
    summed = lax.psum(picked, "space")
    return summed[:, None, :]


def solution(mesh):
    slice_count, space_count = mesh.shape["tm"], mesh.shape["space"]
    slice_bits, space_bits = slice_count.bit_length() - 1, space_count.bit_length() - 1
    on_device = by_collectives
    if (slice_count, space_count) == (1 << slice_bits, 1 << space_bits):
        if slice_bits > 2 and space_bits == 2:
            on_device = functools.partial(by_exchanges, slice_count, space_count)
    return jax.shard_map(
        on_device,
        mesh=mesh,
        in_specs=(
            P(None, None, "tm", "space", None),
            P(None, None, "tm", "space", None),
            P("tm", None, None, None, None),
            P("tm", None),
            P("tm", None),
        ),
        out_specs=P(None, "tm", None),
        check_vma=False,
    )
```
